32 devices in a mesh: groups: 2 (over x), ctx: 8 (over z, y), tp: 2 (over core).
Axes of the slice: x: 2, y: 2, z: 4, core: 2. Of those that a mesh axis runs over, the one named last changes fastest.
Arguments:
- query: bfloat16 [2048, 16384], P(('groups', 'ctx'), 'tp'), parts along dimension 0, may hold values from -600 to 600
- key_input: bfloat16 [2048, 1024], P(('groups', 'ctx'), 'tp'), parts along dimension 0, may hold values from -6 to 6
- value: bfloat16 [2048, 1024], P(('groups', 'ctx'), 'tp'), parts along dimension 0, may hold values from -6 to 6
- upstream: bfloat16 [2048, 16384], P(('groups', 'ctx'), 'tp'), parts along dimension 0, may hold values from -0.119628906 to 0.119628906
- output_gradient: bfloat16 [2048, 16384], P(('groups', 'ctx'), 'tp'), parts along dimension 0, may hold values from -0.119628906 to 0.119628906
- down_adapter: bfloat16 [16384, 32], P('tp'), may hold values from -0.046875 to 0.046875
- up_adapter: bfloat16 [32, 16384], P(None, 'tp'), may hold values from -1 to 1
- document_length_list: int32 [64], P('groups'), parts along dimension 0, may hold values from 1 to 64, 1024 in all
Outputs:
- query_gradient_full: bfloat16 [2048, 16384], P(('groups', 'ctx'), 'tp'), parts along dimension 0
- key_gradient_full: bfloat16 [2048, 1024], P(('groups', 'ctx'), 'tp'), parts along dimension 0
- value_gradient_full: bfloat16 [2048, 1024], P(('groups', 'ctx'), 'tp'), parts along dimension 0
- down_adapter_gradient: float32 [32768, 32], P(('groups', 'tp')), parts along dimension 0
- up_adapter_gradient: float32 [64, 16384], P('groups', 'tp'), parts along dimension 0
The draws below stay inside these ranges and needn't reach their ends.
There are 2 independent parts, one for each index of `groups`. The reference program is written for one: setup_inputs(seed, part) draws one part's arguments, and reference() takes and returns one part's arrays. A program takes and returns all parts, laid end to end along the dimension named above; an argument that names none is the same for every part. Nothing has to cross between parts.
Inputs may be any that keep to these rules, and one draw needn't show every extreme that they name: `document_length_list`: lengths of 32 documents that together fill all 1024 positions; the longest is exactly 64.
All inputs are finite; a program needn't handle non-finite values.
Results may differ from the reference program's by a relative error of at most 0.012.
The reference program's roundings to bfloat16 on the way count: a program that leaves them out, or rounds other values in their place, can miss the bound.
Values may be sent and summed in bfloat16 or wider, within the bound.
A program may use at most 128 MiB of HBM per device.

```python
import math
import jax
import jax.numpy as jnp
import numpy as np
from jax import lax

MODEL_WIDTH = 16384
QUERY_HEADS = 128
KEY_VALUE_HEADS = 8
HEAD_SIZE = 128
ADAPTER_RANK = 32
DEVICE_TOKENS = 128
PACK_TOKENS = 1024
STRETCH = 64
NCHUNK = 16
NDOC = 32
N_CTX = 8


def draw_query(key, part):
    key = jax.random.fold_in(key, 7)
    base_key = jax.random.fold_in(key, 0)
    base = jnp.clip(jax.random.normal(base_key, (PACK_TOKENS, QUERY_HEADS * HEAD_SIZE), jnp.float32), -6.0, 6.0)
    return base.astype(jnp.bfloat16)


def steps_of(own_key, dims, pieces, least, top_value):
    def one(axis_at, blocks):
        steps = jax.random.uniform(jax.random.fold_in(jax.random.fold_in(own_key, 6), axis_at), (blocks,), jnp.float32, least / len(pieces), top_value / len(pieces))
        return jnp.repeat(jnp.exp(steps), dims[axis_at] // blocks).reshape((-1,) + (1,) * (len(dims) - axis_at - 1))

    factor_of = one(*pieces[0])
    for cut in pieces[1:]:
        factor_of = factor_of * one(*cut)
    return factor_of


def split_up(number_of, total, limit, lean):
    loads = [(1 << 20) // math.isqrt(grade ** lean) + 1 for grade in range(2, number_of + 1)]
    surplus, counts = total - limit - (number_of - 1), [1] * (number_of - 1)
    while surplus > 0:
        candidates = [i for i in range(number_of - 1) if counts[i] < limit]
        pool, remaining = sum([loads[i] for i in candidates]), surplus
        for i in candidates:
            extra = min(limit - counts[i], max(1, remaining * loads[i] // pool), surplus)
            counts[i] = counts[i] + extra
            surplus = surplus - extra
    return np.array([limit] + counts)


def uneven(own_key, number_of, total, limit, lean):
    if number_of == 2:
        one = jax.random.randint(own_key, (), max(1, total - limit), min(limit, total - 1) + 1)
        return jnp.stack([one, total - one])
    sizes = jnp.asarray(split_up(number_of, total, limit, lean), jnp.int32)
    pairs = (number_of - 1) // 2
    donor, taker = sizes[1:1 + 2 * pairs:2], sizes[2:2 + 2 * pairs:2]
    margin = jnp.minimum(donor - 1, limit - taker)
    passed = jax.random.randint(jax.random.fold_in(own_key, 1), (pairs,), 0, 1 << 20) % (margin + 1)
    sizes = sizes.at[1:1 + 2 * pairs:2].set(donor - passed).at[2:2 + 2 * pairs:2].set(taker + passed)
    return sizes[jax.random.permutation(jax.random.fold_in(own_key, 2), number_of)]


def normal_values(rng, dims, scale, bound, cuts=(), kind=jnp.bfloat16):
    entries = jax.random.normal(rng, dims, jnp.float32) * scale
    if len(cuts) > 0:
        entries = steps_of(rng, dims, cuts, -0.22, 0.18) * entries
    return jnp.clip(entries, min=-bound, max=bound).astype(kind)


def setup_inputs(seed: int = 0, part: int = 0) -> dict:
    arg_keys = jax.random.split(jax.random.key(seed), 9)
    own_keys = jax.random.split(jax.random.fold_in(arg_keys[8], part), 9)
    return {
        "query": draw_query(jax.random.fold_in(jax.random.fold_in(arg_keys[8], part), 71), part),
        "key_input": normal_values(own_keys[1], (PACK_TOKENS, KEY_VALUE_HEADS * HEAD_SIZE), 1.0, 6.0, ((0, 8), (1, 2))),
        "value": normal_values(own_keys[2], (PACK_TOKENS, KEY_VALUE_HEADS * HEAD_SIZE), 1.0, 6.0, ((0, 8), (1, 2))),
        "upstream": normal_values(own_keys[3], (PACK_TOKENS, QUERY_HEADS * HEAD_SIZE), 0.02, 0.119628906, ((0, 8), (1, 2))),
        "output_gradient": normal_values(own_keys[4], (PACK_TOKENS, MODEL_WIDTH), 0.02, 0.119628906, ((0, 8), (1, 2))),
        "down_adapter": normal_values(arg_keys[5], (QUERY_HEADS * HEAD_SIZE, ADAPTER_RANK), (QUERY_HEADS * HEAD_SIZE) ** -0.5, 0.046875, ((0, 2),)),
        "up_adapter": normal_values(arg_keys[6], (ADAPTER_RANK, MODEL_WIDTH), ADAPTER_RANK ** -0.5, 1.0, ((1, 2),)),
        "document_length_list": uneven(own_keys[7], NDOC, PACK_TOKENS, STRETCH, 2).astype(jnp.int32),
    }


NEG = -1.0e30
ADAPTER_SCALE = 0.5


def lowered(tensor):
    return lax.optimization_barrier(tensor.astype(jnp.bfloat16))


def reference(query, key_input, value, upstream, output_gradient, down_adapter, up_adapter, document_length_list):
    query_group_size = QUERY_HEADS // KEY_VALUE_HEADS
    score_scale = HEAD_SIZE ** -0.5
    rows = jnp.arange(PACK_TOKENS, dtype=jnp.int32)
    device = rows // DEVICE_TOKENS
    offset = rows % DEVICE_TOKENS
    stretch_index = jnp.where(offset < STRETCH, device, NCHUNK - 1 - device)
    token_position = (stretch_index * STRETCH + offset % STRETCH).astype(jnp.int32)
    pos_stretch = rows // STRETCH
    pos_device = jnp.where(pos_stretch < N_CTX, pos_stretch, NCHUNK - 1 - pos_stretch)
    pos_inner = jnp.where(pos_stretch < N_CTX, rows % STRETCH, STRETCH + rows % STRETCH)
    position_row_lookup = (pos_device * DEVICE_TOKENS + pos_inner).astype(jnp.int32)
    lengths = document_length_list.astype(jnp.int32)
    starts = (jnp.cumsum(lengths) - lengths).astype(jnp.int32)
    doc_of_pos = (jnp.sum((starts[None, :] <= rows[:, None]).astype(jnp.int32), axis=1) - 1).astype(jnp.int32)

    inner_product = jnp.dot(output_gradient, up_adapter.T, preferred_element_type=jnp.float32)
    inner_lower = lowered(inner_product)
    attention_gradient = (upstream.astype(jnp.float32) + ADAPTER_SCALE * jnp.dot(inner_lower, down_adapter.T, preferred_element_type=jnp.float32)).astype(jnp.bfloat16)

    query_position = jnp.take(query, position_row_lookup, axis=0)
    position_gradient = jnp.take(attention_gradient, position_row_lookup, axis=0)
    key_padded = jnp.concatenate([jnp.zeros((DEVICE_TOKENS, KEY_VALUE_HEADS * HEAD_SIZE), jnp.bfloat16), jnp.take(key_input, position_row_lookup, axis=0)], axis=0)
    value_padded = jnp.concatenate([jnp.zeros((DEVICE_TOKENS, KEY_VALUE_HEADS * HEAD_SIZE), jnp.bfloat16), jnp.take(value, position_row_lookup, axis=0)], axis=0)
    doc_pad = jnp.concatenate([jnp.full((DEVICE_TOKENS,), -1, jnp.int32), doc_of_pos]).astype(jnp.int32)

    def one_block(carry, block_number):
        key_accumulator, value_accumulator = carry
        start_index = (block_number * DEVICE_TOKENS).astype(jnp.int32)
        query_tile_block = lax.dynamic_slice_in_dim(query_position, start_index, DEVICE_TOKENS, 0).astype(jnp.float32).reshape(DEVICE_TOKENS, KEY_VALUE_HEADS, query_group_size, HEAD_SIZE)
        key_slice_window = lax.dynamic_slice_in_dim(key_padded, start_index, 2 * DEVICE_TOKENS, 0).astype(jnp.float32).reshape(2 * DEVICE_TOKENS, KEY_VALUE_HEADS, HEAD_SIZE)
        value_slice_window = lax.dynamic_slice_in_dim(value_padded, start_index, 2 * DEVICE_TOKENS, 0).astype(jnp.float32).reshape(2 * DEVICE_TOKENS, KEY_VALUE_HEADS, HEAD_SIZE)
        block_gradient = lax.dynamic_slice_in_dim(position_gradient, start_index, DEVICE_TOKENS, 0).astype(jnp.float32).reshape(DEVICE_TOKENS, KEY_VALUE_HEADS, query_group_size, HEAD_SIZE)
        query_doc = lax.dynamic_slice_in_dim(doc_of_pos, start_index, DEVICE_TOKENS, 0)
        key_doc = lax.dynamic_slice_in_dim(doc_pad, start_index, 2 * DEVICE_TOKENS, 0)
        query_spot = start_index + jnp.arange(DEVICE_TOKENS, dtype=jnp.int32)
        key_spot = start_index - DEVICE_TOKENS + jnp.arange(2 * DEVICE_TOKENS, dtype=jnp.int32)
        allowed = jnp.logical_and(query_doc[:, None] == key_doc[None, :], key_spot[None, :] <= query_spot[:, None])
        scores = jnp.einsum("qkgd,skd->kgqs", query_tile_block, key_slice_window) * score_scale
        scores = jnp.where(allowed[None, None], scores, NEG)
        row_top = jnp.max(scores, axis=-1, keepdims=True)
        expo = jnp.exp(scores - row_top)
        prob_full = expo / jnp.sum(expo, axis=-1, keepdims=True)
        prob_low = lowered(prob_full).astype(jnp.float32)
        attn_block = lowered(jnp.einsum("kgqs,skd->qkgd", prob_low, value_slice_window))
        row_delta = jnp.sum(block_gradient * attn_block.astype(jnp.float32), axis=-1).transpose(1, 2, 0)
        dprobs = jnp.einsum("qkgd,skd->kgqs", block_gradient, value_slice_window)
        dscores = lowered(prob_full * (dprobs - row_delta[..., None])).astype(jnp.float32)
        query_grad = (score_scale * jnp.einsum("kgqs,skd->qkgd", dscores, key_slice_window)).astype(jnp.bfloat16)
        key_grad = score_scale * jnp.einsum("kgqs,qkgd->skd", dscores, query_tile_block)
        value_grad = jnp.einsum("kgqs,qkgd->skd", prob_low, block_gradient)
        key_accumulator = lax.dynamic_update_slice_in_dim(key_accumulator, lax.dynamic_slice_in_dim(key_accumulator, start_index, 2 * DEVICE_TOKENS, 0) + key_grad, start_index, 0)
        value_accumulator = lax.dynamic_update_slice_in_dim(value_accumulator, lax.dynamic_slice_in_dim(value_accumulator, start_index, 2 * DEVICE_TOKENS, 0) + value_grad, start_index, 0)
        return (key_accumulator, value_accumulator), (attn_block.reshape(DEVICE_TOKENS, QUERY_HEADS * HEAD_SIZE), query_grad.reshape(DEVICE_TOKENS, QUERY_HEADS * HEAD_SIZE))

    empty_result = jnp.zeros((PACK_TOKENS + DEVICE_TOKENS, KEY_VALUE_HEADS, HEAD_SIZE), jnp.float32)
    carry, stacked = lax.scan(one_block, (empty_result, empty_result), jnp.arange(PACK_TOKENS // DEVICE_TOKENS, dtype=jnp.int32))
    key_accumulator, value_accumulator = carry
    attn_blocks, query_blocks = stacked
    attention_rows = jnp.take(attn_blocks.reshape(PACK_TOKENS, QUERY_HEADS * HEAD_SIZE), token_position, axis=0)
    query_gradient_full = jnp.take(query_blocks.reshape(PACK_TOKENS, QUERY_HEADS * HEAD_SIZE), token_position, axis=0)
    key_gradient_full = jnp.take(key_accumulator[DEVICE_TOKENS:].reshape(PACK_TOKENS, KEY_VALUE_HEADS * HEAD_SIZE), token_position, axis=0).astype(jnp.bfloat16)
    value_gradient_full = jnp.take(value_accumulator[DEVICE_TOKENS:].reshape(PACK_TOKENS, KEY_VALUE_HEADS * HEAD_SIZE), token_position, axis=0).astype(jnp.bfloat16)

    outer_lower = jnp.dot(attention_rows, down_adapter, preferred_element_type=jnp.float32).astype(jnp.bfloat16)
    down_adapter_gradient = ADAPTER_SCALE * jnp.dot(attention_rows.T, inner_lower, preferred_element_type=jnp.float32)
    up_adapter_gradient = ADAPTER_SCALE * jnp.dot(outer_lower.T, output_gradient, preferred_element_type=jnp.float32)
    return query_gradient_full, key_gradient_full, value_gradient_full, down_adapter_gradient, up_adapter_gradient
```

```python
import functools

import jax
import jax.numpy as jnp
from jax import lax
from jax.experimental import pallas as pl
from jax.experimental.pallas import tpu as pltpu
from jax.sharding import PartitionSpec as P

HEAD_SIZE = 128
NEG = -1e30
ADAPTER_SCALE = 0.5
MESH = pl.DeviceIdType.MESH
F32 = jnp.float32
BF16 = jnp.bfloat16


def dot(a, b, contract):
    return lax.dot_general(a, b, (contract, ((), ())), preferred_element_type=F32)


def nn(a, b):
    return dot(a, b, ((1,), (0,)))


def nt(a, b):
    return dot(a, b, ((1,), (1,)))


def tn(a, b):
    return dot(a, b, ((0,), (0,)))


def kernel(
    ctx_size, query_hbm, key_hbm, value_hbm, upstream_hbm, grad_hbm, down_hbm, up_hbm, lengths_ref,
    dquery_hbm, dkey_ref, dvalue_ref, ddown_ref, dup_ref,
    query, upstream, grad, down, up, keys, values, bias, probs, attn, dquery,
    low_send, low_recv, low, low_t, outer_send, outer_recv,
    own_dkv, back_send, back_recv, acc, part_send, part_recv, total,
    load_sem, store_sem, halo_send_sem, halo_recv_sem, low_sem, back_sem, step_send_sem, step_recv_sem,
):
    rows, width = query.shape
    half = rows // 2
    kv_width = keys.shape[2]
    kv_heads = kv_width // HEAD_SIZE
    group = width // kv_width
    group_width = group * HEAD_SIZE
    scale = HEAD_SIZE ** (-0.5)
    levels = ctx_size.bit_length() - 1
    me = lax.axis_index("ctx")
    tp = lax.axis_index("tp")
    first = me == 0
    last = me == ctx_size - 1
    bits = [(me // (1 << b)) % 2 for b in range(levels)]
    partners = [me + (1 << b) * (1 - 2 * bits[b]) for b in range(levels)]
    orders = [list(range(levels)), list(range(levels))]
    for i in range(0, levels - 1, 2):
        orders[0][i], orders[0][i + 1] = i + 1, i

    loads = []
    for i, (src, dst) in enumerate(
        [
            (grad_hbm, grad),
            (up_hbm, up),
            (query_hbm, query),
            (key_hbm.at[0:half], keys.at[0, half:rows]),
            (key_hbm.at[half:rows], keys.at[1, half:rows]),
            (value_hbm.at[0:half], values.at[0, half:rows]),
            (value_hbm.at[half:rows], values.at[1, half:rows]),
            (down_hbm, down),
            (upstream_hbm, upstream),
        ]
    ):
        copy = pltpu.make_async_copy(src, dst, load_sem.at[i])
        copy.start()
        loads.append(copy)

    barrier = pltpu.get_barrier_semaphore()
    pl.semaphore_signal(barrier, inc=1, device_id={"tp": 1 - tp}, device_id_type=MESH)
    for partner in partners:
        pl.semaphore_signal(barrier, inc=1, device_id={"ctx": partner}, device_id_type=MESH)

    @pl.when(jnp.logical_not(first))
    def _():
        pl.semaphore_signal(barrier, inc=1, device_id={"ctx": me - 1}, device_id_type=MESH)

    @pl.when(jnp.logical_not(last))
    def _():
        pl.semaphore_signal(barrier, inc=1, device_id={"ctx": me + 1}, device_id_type=MESH)

    lengths = lengths_ref[...].astype(F32)
    docs = lengths.shape[1]
    line = lax.broadcasted_iota(jnp.int32, (docs, docs), 0)
    column = lax.broadcasted_iota(jnp.int32, (docs, docs), 1)
    tall = jnp.sum(jnp.where(line == column, lengths, 0.0), axis=1, keepdims=True)
    starts = jnp.sum(jnp.where(line < column, tall, 0.0), axis=0, keepdims=True)
    for t in range(2):
        stretch = me if t == 0 else 2 * ctx_size - 1 - me
        spot = (lax.broadcasted_iota(jnp.int32, (half, 1), 0) + stretch * half).astype(F32)
        begin = jnp.max(jnp.where(starts <= spot, starts, -1.0), axis=1, keepdims=True)
        key_spot = (
            lax.broadcasted_iota(jnp.int32, (half, rows), 1) + (stretch - 1) * half
        ).astype(F32)
        allowed = jnp.logical_and(key_spot >= begin, key_spot <= spot)
        bias[t] = jnp.where(allowed, 0.0, NEG)

    pl.semaphore_wait(
        barrier, 1 + levels + jnp.where(first, 0, 1) + jnp.where(last, 0, 1)
    )

    def halo(hbm, buffer, which, t):
        part = hbm.at[0:half] if t == 0 else hbm.at[half:rows]
        target = me + 1 if t == 0 else me - 1
        return pltpu.make_async_remote_copy(
            src_ref=part,
            dst_ref=buffer.at[t, 0:half],
            send_sem=halo_send_sem.at[which, t],
            recv_sem=halo_recv_sem.at[which, t],
            device_id={"ctx": target},
            device_id_type=MESH,
        )

    halos = [halo(key_hbm, keys, 0, t) for t in range(2)] + [
        halo(value_hbm, values, 1, t) for t in range(2)
    ]

    @pl.when(jnp.logical_not(last))
    def _():
        halos[0].start()
        halos[2].start()

    @pl.when(jnp.logical_not(first))
    def _():
        halos[1].start()
        halos[3].start()

    loads[0].wait()
    loads[1].wait()
    low_send[...] = nt(grad[...], up[...]).T
    low_copy = pltpu.make_async_remote_copy(
        src_ref=low_send, dst_ref=low_recv, send_sem=low_sem.at[0], recv_sem=low_sem.at[1],
        device_id={"tp": 1 - tp}, device_id_type=MESH,
    )
    low_copy.start()

    for i in range(2, 8):
        loads[i].wait()

    @pl.when(first)
    def _():
        keys[0, 0:half] = jnp.zeros((half, kv_width), BF16)
        values[0, 0:half] = jnp.zeros((half, kv_width), BF16)

    @pl.when(jnp.logical_not(first))
    def _():
        halos[0].wait_recv()
        halos[2].wait_recv()

    @pl.when(last)
    def _():
        keys[1, 0:half] = keys[0, half:rows]
        values[1, 0:half] = values[0, half:rows]

    @pl.when(jnp.logical_not(last))
    def _():
        halos[1].wait_recv()
        halos[3].wait_recv()

    def stacked(ref, t, g):
        return jnp.concatenate(
            [
                ref[t * half : (t + 1) * half, g * group_width + h * HEAD_SIZE : g * group_width + (h + 1) * HEAD_SIZE]
                for h in range(group)
            ],
            axis=0,
        )

    def unstack(ref, t, g, block):
        for h in range(group):
            start = g * group_width + h * HEAD_SIZE
            ref[t * half : (t + 1) * half, start : start + HEAD_SIZE] = block[h * half : (h + 1) * half]

    outer = jnp.zeros((rows, low_send.shape[0]), F32)
    for g in range(kv_heads):
        head = slice(g * HEAD_SIZE, (g + 1) * HEAD_SIZE)
        for t in range(2):
            scores = nt(stacked(query, t, g), keys[t, :, head]) * scale
            scores = scores.reshape(group, half, rows) + bias[t][None]
            scores = scores.reshape(group * half, rows)
            expo = jnp.exp(scores - jnp.max(scores, axis=1, keepdims=True))
            prob = expo * (1.0 / jnp.sum(expo, axis=1, keepdims=True))
            probs[2 * g + t] = prob
            out = nn(prob.astype(BF16), values[t, :, head]).astype(BF16)
            unstack(attn, t, g, out)
        columns = slice(g * group_width, (g + 1) * group_width)
        outer = outer + nt(attn[:, columns], down[:, columns])
    outer_send[...] = outer.T
    outer_copy = pltpu.make_async_remote_copy(
        src_ref=outer_send, dst_ref=outer_recv, send_sem=low_sem.at[2], recv_sem=low_sem.at[3],
        device_id={"tp": 1 - tp}, device_id_type=MESH,
    )
    outer_copy.start()

    slot_width = acc.shape[3]
    started = []

    def ranges(which):
        bases = [0]
        for s in range(levels):
            bases.append(bases[-1] + bits[orders[which][s]] * (ctx_size >> (s + 1)))
        return bases

    bases = [ranges(0), ranges(1)]

    def begin_step(which, step):
        if step < levels:
            s = step
            size = ctx_size >> (s + 1)
            bit = bits[orders[which][s]]
            away = bases[which][s] + (1 - bit) * size
            part_send[which, pl.ds(away, size)] = acc[which, pl.ds(away, size)].astype(BF16)
            src = part_send.at[which, pl.ds(away, size)]
            offset = ctx_size - (ctx_size >> s)
            dst = part_recv.at[which, pl.ds(offset, size)]
        else:
            s = 2 * levels - 1 - step
            size = ctx_size >> (s + 1)
            if step == levels:
                mine = bases[which][levels]
                total[which, pl.ds(mine, 1)] = acc[which, pl.ds(mine, 1)].astype(BF16)
            src = total.at[which, pl.ds(bases[which][s + 1], size)]
            dst = src
        copy = pltpu.make_async_remote_copy(
            src_ref=src, dst_ref=dst,
            send_sem=step_send_sem.at[which, step], recv_sem=step_recv_sem.at[which, step],
            device_id={"ctx": partners[orders[which][s]]}, device_id_type=MESH,
        )
        copy.start()
        started.append(copy)
        return copy

    def end_step(which, step, copy):
        copy.wait_recv()
        if step < levels:
            size = ctx_size >> (step + 1)
            offset = ctx_size - (ctx_size >> step)
            keep = pl.ds(bases[which][step + 1], size)
            acc[which, keep] = acc[which, keep] + part_recv[which, pl.ds(offset, size)].astype(F32)

    low_copy.wait_recv()
    low_sum = (low_send[...] + low_recv[...]).astype(BF16)
    low_t[...] = low_sum
    low[...] = (low_send[...] + low_recv[...]).T.astype(BF16)
    for i in range(ctx_size):
        acc[0, i] = ADAPTER_SCALE * nn(low_sum, attn[:, i * slot_width : (i + 1) * slot_width])
    flying = [begin_step(0, 0)]
    outer_copy.wait_recv()
    outer_sum = (outer_send[...] + outer_recv[...]).astype(BF16)
    for i in range(ctx_size):
        acc[1, i] = ADAPTER_SCALE * nn(outer_sum, grad[:, i * slot_width : (i + 1) * slot_width])
    flying.append(begin_step(1, 0))
    loads[8].wait()

    stores = []

    def backward(g):
        head = slice(g * HEAD_SIZE, (g + 1) * HEAD_SIZE)
        tail = slice(kv_width + g * HEAD_SIZE, kv_width + (g + 1) * HEAD_SIZE)
        columns = slice(g * group_width, (g + 1) * group_width)
        upstream[:, columns] = (
            upstream[:, columns].astype(F32) + ADAPTER_SCALE * nn(low[...], down[:, columns])
        ).astype(BF16)
        for t in range(2):
            dout = stacked(upstream, t, g)
            out = stacked(attn, t, g)
            delta = jnp.sum(dout.astype(F32) * out.astype(F32), axis=1, keepdims=True)
            prob = probs[2 * g + t]
            dscores = (prob * (nt(dout, values[t, :, head]) - delta)).astype(BF16)
            dq = (nn(dscores, keys[t, :, head]) * scale).astype(BF16)
            unstack(dquery, t, g, dq)
            dk = tn(dscores, stacked(query, t, g)) * scale
            dv = tn(prob.astype(BF16), dout)
            back_send[t, :, head] = dk[0:half].astype(BF16)
            back_send[t, :, tail] = dv[0:half].astype(BF16)
            own_dkv[t, :, head] = dk[half:rows]
            own_dkv[t, :, tail] = dv[half:rows]
        store = pltpu.make_async_copy(
            dquery.at[:, columns], dquery_hbm.at[:, columns], store_sem.at[g]
        )
        store.start()
        stores.append(store)

    backs = []

    def send_back():
        for t in range(2):
            backs.append(
                pltpu.make_async_remote_copy(
                    src_ref=back_send.at[t], dst_ref=back_recv.at[t],
                    send_sem=back_sem.at[0, t], recv_sem=back_sem.at[1, t],
                    device_id={"ctx": me - 1 if t == 0 else me + 1}, device_id_type=MESH,
                )
            )

        @pl.when(jnp.logical_not(first))
        def _():
            backs[0].start()

        @pl.when(jnp.logical_not(last))
        def _():
            backs[1].start()

        @pl.when(first)
        def _():
            back_recv[1] = jnp.zeros(back_recv.shape[1:], BF16)

        @pl.when(last)
        def _():
            back_recv[0] = back_send[1]

    for step in range(2 * levels):
        if step < kv_heads:
            backward(step)
            if step == kv_heads - 1:
                send_back()
        for which in range(2):
            end_step(which, step, flying[which])
            if step + 1 < 2 * levels:
                flying[which] = begin_step(which, step + 1)
    for g in range(2 * levels, kv_heads):
        backward(g)
    if kv_heads > 2 * levels:
        send_back()

    for i in range(ctx_size):
        columns = slice(i * slot_width, (i + 1) * slot_width)
        ddown_ref[:, columns] = total[0, i].astype(F32)
        dup_ref[:, columns] = total[1, i].astype(F32)

    @pl.when(jnp.logical_not(last))
    def _():
        backs[0].wait_recv()

    @pl.when(jnp.logical_not(first))
    def _():
        backs[1].wait_recv()

    for t in range(2):
        both = own_dkv[t] + back_recv[t].astype(F32)
        dkey_ref[t * half : (t + 1) * half] = both[:, :kv_width].astype(BF16)
        dvalue_ref[t * half : (t + 1) * half] = both[:, kv_width:].astype(BF16)

    for store in stores:
        store.wait()
    for copy in started:
        copy.wait_send()
    low_copy.wait_send()
    outer_copy.wait_send()

    @pl.when(jnp.logical_not(last))
    def _():
        halos[0].wait_send()
        halos[2].wait_send()
        backs[1].wait_send()

    @pl.when(jnp.logical_not(first))
    def _():
        halos[1].wait_send()
        halos[3].wait_send()
        backs[0].wait_send()


def shards(
    query,
    key_input,
    value,
    upstream,
    output_gradient,
    down_adapter,
    up_adapter,
    document_length_list,
):
    rows, width = query.shape
    kv_width = key_input.shape[1]
    kv_heads = kv_width // HEAD_SIZE
    group = width // kv_width
    rank, model = up_adapter.shape
    half = rows // 2
    ctx_size = lax.axis_size("ctx")
    levels = ctx_size.bit_length() - 1
    slot = (ctx_size, rank, width // ctx_size)
    anywhere = pl.BlockSpec(memory_space=pl.ANY)
    vmem = pl.BlockSpec(memory_space=pltpu.VMEM)
    dma = pltpu.SemaphoreType.DMA
    outs = pl.pallas_call(
        functools.partial(kernel, ctx_size),
        out_shape=(
            jax.ShapeDtypeStruct((rows, width), BF16),
            jax.ShapeDtypeStruct((rows, kv_width), BF16),
            jax.ShapeDtypeStruct((rows, kv_width), BF16),
            jax.ShapeDtypeStruct((rank, width), F32),
            jax.ShapeDtypeStruct((rank, model), F32),
        ),
        in_specs=[anywhere] * 7 + [vmem],
        out_specs=(anywhere, vmem, vmem, vmem, vmem),
        scratch_shapes=[
            pltpu.VMEM((rows, width), BF16),
            pltpu.VMEM((rows, width), BF16),
            pltpu.VMEM((rows, model), BF16),
            pltpu.VMEM((rank, width), BF16),
            pltpu.VMEM((rank, model), BF16),
            pltpu.VMEM((2, rows, kv_width), BF16),
            pltpu.VMEM((2, rows, kv_width), BF16),
            pltpu.VMEM((2, half, rows), F32),
            pltpu.VMEM((2 * kv_heads, group * half, rows), F32),
            pltpu.VMEM((rows, width), BF16),
            pltpu.VMEM((rows, width), BF16),
            pltpu.VMEM((rank, rows), F32),
            pltpu.VMEM((rank, rows), F32),
            pltpu.VMEM((rows, rank), BF16),
            pltpu.VMEM((rank, rows), BF16),
            pltpu.VMEM((rank, rows), F32),
            pltpu.VMEM((rank, rows), F32),
            pltpu.VMEM((2, half, 2 * kv_width), F32),
            pltpu.VMEM((2, half, 2 * kv_width), BF16),
            pltpu.VMEM((2, half, 2 * kv_width), BF16),
            pltpu.VMEM((2,) + slot, F32),
            pltpu.VMEM((2,) + slot, BF16),
            pltpu.VMEM((2,) + slot, BF16),
            pltpu.VMEM((2,) + slot, BF16),
            dma((9,)),
            dma((kv_heads,)),
            dma((2, 2)),
            dma((2, 2)),
            dma((4,)),
            dma((2, 2)),
            dma((2, 2 * levels)),
            dma((2, 2 * levels)),
        ],
        compiler_params=pltpu.CompilerParams(
            collective_id=0, has_side_effects=True, vmem_limit_bytes=48 * 1024 * 1024
        ),
    )(
        query, key_input, value, upstream, output_gradient, down_adapter.T, up_adapter,
        document_length_list[None, :],
    )
    dquery, dkey, dvalue, ddown, dup = outs
    return dquery, dkey, dvalue, ddown.T, dup


def solution(mesh):
    in_specs = (
        P(("groups", "ctx"), "tp"),
        P(("groups", "ctx"), "tp"),
        P(("groups", "ctx"), "tp"),
        P(("groups", "ctx"), "tp"),
        P(("groups", "ctx"), "tp"),
        P("tp", None),
        P(None, "tp"),
        P("groups"),
    )
    out_specs = (
        P(("groups", "ctx"), "tp"),
        P(("groups", "ctx"), "tp"),
        P(("groups", "ctx"), "tp"),
        P(("groups", "tp"), None),
        P("groups", "tp"),
    )
    return jax.shard_map(shards, mesh=mesh, in_specs=in_specs, out_specs=out_specs, check_vma=False)
```

```python
import functools

import jax
import jax.numpy as jnp
from jax import lax
from jax.experimental import pallas as pl
from jax.experimental.pallas import tpu as pltpu
from jax.sharding import PartitionSpec as P

HEAD_SIZE = 128
NEG = -1e30
ADAPTER_SCALE = 0.5
MESH = pl.DeviceIdType.MESH
F32 = jnp.float32
BF16 = jnp.bfloat16


def dot(a, b, contract):
    return lax.dot_general(a, b, (contract, ((), ())), preferred_element_type=F32)


def nn(a, b):
    return dot(a, b, ((1,), (0,)))


def nt(a, b):
    return dot(a, b, ((1,), (1,)))


def tn(a, b):
    return dot(a, b, ((0,), (0,)))


def kernel(
    ctx_size, query_hbm, key_hbm, value_hbm, upstream_hbm, grad_hbm, down_hbm, up_hbm, lengths_hbm,
    dquery_hbm, dkey_ref, dvalue_ref, total,
    query, upstream, grad, down, up, keys, values, bias, probs, attn, dquery,
    low_send, low_recv, low, outer_send, outer_recv,
    own_dkv, back_send, back_recv, acc, part_send, part_recv, lengths_vmem,
    load_sem, store_sem, halo_send_sem, halo_recv_sem, low_sem, back_sem, step_send_sem, step_recv_sem,
):
    rows, width = query.shape
    half = rows // 2
    kv_width = keys.shape[2]
    kv_heads = kv_width // HEAD_SIZE
    group = width // kv_width
    group_width = group * HEAD_SIZE
    scale = HEAD_SIZE ** (-0.5)
    levels = ctx_size.bit_length() - 1
    me = lax.axis_index("ctx")
    tp = lax.axis_index("tp")
    first = me == 0
    last = me == ctx_size - 1
    bits = [(me // (1 << b)) % 2 for b in range(levels)]
    partners = [me + (1 << b) * (1 - 2 * bits[b]) for b in range(levels)]
    cuts = acc.shape[0] // 2
    swapped = list(range(levels))
    for i in range(0, levels - 1, 2):
        swapped[i], swapped[i + 1] = i + 1, i
    orders = [
        swapped if w < cuts and w % 2 == 0 or w == cuts + 1 else list(range(levels))
        for w in range(2 * cuts)
    ]

    loads = []
    for i, (src, dst) in enumerate(
        [
            (grad_hbm, grad),
            (up_hbm, up),
            (query_hbm, query),
            (key_hbm.at[0:half], keys.at[0, half:rows]),
            (key_hbm.at[half:rows], keys.at[1, half:rows]),
            (value_hbm.at[0:half], values.at[0, half:rows]),
            (value_hbm.at[half:rows], values.at[1, half:rows]),
            (down_hbm, down),
            (upstream_hbm, upstream),
            (lengths_hbm, lengths_vmem),
        ]
    ):
        copy = pltpu.make_async_copy(src, dst, load_sem.at[i])
        copy.start()
        loads.append(copy)

    barrier = pltpu.get_barrier_semaphore()
    pl.semaphore_signal(barrier, inc=1, device_id={"tp": 1 - tp}, device_id_type=MESH)
    for partner in partners:
        pl.semaphore_signal(barrier, inc=1, device_id={"ctx": partner}, device_id_type=MESH)

    @pl.when(jnp.logical_not(first))
    def _():
        pl.semaphore_signal(barrier, inc=1, device_id={"ctx": me - 1}, device_id_type=MESH)

    @pl.when(jnp.logical_not(last))
    def _():
        pl.semaphore_signal(barrier, inc=1, device_id={"ctx": me + 1}, device_id_type=MESH)

    loads[9].wait()
    lengths = lengths_vmem[...].astype(F32)
    docs = lengths.shape[1]
    line = lax.broadcasted_iota(jnp.int32, (docs, docs), 0)
    column = lax.broadcasted_iota(jnp.int32, (docs, docs), 1)
    tall = jnp.sum(jnp.where(line == column, lengths, 0.0), axis=1, keepdims=True)
    starts = jnp.sum(jnp.where(line < column, tall, 0.0), axis=0, keepdims=True)
    for t in range(2):
        stretch = me if t == 0 else 2 * ctx_size - 1 - me
        spot = (lax.broadcasted_iota(jnp.int32, (half, 1), 0) + stretch * half).astype(F32)
        begin = jnp.max(jnp.where(starts <= spot, starts, -1.0), axis=1, keepdims=True)
        key_spot = (
            lax.broadcasted_iota(jnp.int32, (half, rows), 1) + (stretch - 1) * half
        ).astype(F32)
        allowed = jnp.logical_and(key_spot >= begin, key_spot <= spot)
        bias[t] = jnp.where(allowed, 0.0, NEG)

    pl.semaphore_wait(
        barrier, 1 + levels + jnp.where(first, 0, 1) + jnp.where(last, 0, 1)
    )

    def halo(hbm, buffer, which, t):
        part = hbm.at[0:half] if t == 0 else hbm.at[half:rows]
        target = me + 1 if t == 0 else me - 1
        return pltpu.make_async_remote_copy(
            src_ref=part,
            dst_ref=buffer.at[t, 0:half],
            send_sem=halo_send_sem.at[which, t],
            recv_sem=halo_recv_sem.at[which, t],
            device_id={"ctx": target},
            device_id_type=MESH,
        )

    halos = [halo(key_hbm, keys, 0, t) for t in range(2)] + [
        halo(value_hbm, values, 1, t) for t in range(2)
    ]

    @pl.when(jnp.logical_not(last))
    def _():
        halos[0].start()
        halos[2].start()

    @pl.when(jnp.logical_not(first))
    def _():
        halos[1].start()
        halos[3].start()

    loads[0].wait()
    loads[1].wait()
    low_send[...] = nt(grad[...], up[...]).T
    low_copy = pltpu.make_async_remote_copy(
        src_ref=low_send, dst_ref=low_recv, send_sem=low_sem.at[0], recv_sem=low_sem.at[1],
        device_id={"tp": 1 - tp}, device_id_type=MESH,
    )
    low_copy.start()

    for i in range(2, 8):
        loads[i].wait()

    @pl.when(first)
    def _():
        keys[0, 0:half] = jnp.zeros((half, kv_width), BF16)
        values[0, 0:half] = jnp.zeros((half, kv_width), BF16)

    @pl.when(jnp.logical_not(first))
    def _():
        halos[0].wait_recv()
        halos[2].wait_recv()

    @pl.when(last)
    def _():
        keys[1, 0:half] = keys[0, half:rows]
        values[1, 0:half] = values[0, half:rows]

    @pl.when(jnp.logical_not(last))
    def _():
        halos[1].wait_recv()
        halos[3].wait_recv()

    def stacked(ref, t, g):
        return jnp.concatenate(
            [
                ref[t * half : (t + 1) * half, g * group_width + h * HEAD_SIZE : g * group_width + (h + 1) * HEAD_SIZE]
                for h in range(group)
            ],
            axis=0,
        )

    def unstack(ref, t, g, block):
        for h in range(group):
            start = g * group_width + h * HEAD_SIZE
            ref[t * half : (t + 1) * half, start : start + HEAD_SIZE] = block[h * half : (h + 1) * half]

    low_copy.wait_recv()
    low_t = (low_send[...] + low_recv[...]).astype(BF16)
    low[...] = (low_send[...] + low_recv[...]).T.astype(BF16)

    slot_width = acc.shape[3]
    started = []

    def ranges(order):
        bases = [0]
        for s in range(levels):
            bases.append(bases[-1] + bits[order[s]] * (ctx_size >> (s + 1)))
        return bases

    bases = [ranges(order) for order in orders]

    def begin_step(which, step):
        if step < levels:
            s = step
            size = ctx_size >> (s + 1)
            bit = bits[orders[which][s]]
            away = bases[which][s] + (1 - bit) * size
            part_send[which, pl.ds(away, size)] = acc[which, pl.ds(away, size)].astype(BF16)
            src = part_send.at[which, pl.ds(away, size)]
            offset = ctx_size - (ctx_size >> s)
            dst = part_recv.at[which, pl.ds(offset, size)]
        else:
            s = 2 * levels - 1 - step
            size = ctx_size >> (s + 1)
            if step == levels:
                mine = bases[which][levels]
                total[which, pl.ds(mine, 1)] = acc[which, pl.ds(mine, 1)].astype(BF16)
            src = total.at[which, pl.ds(bases[which][s + 1], size)]
            dst = src
        copy = pltpu.make_async_remote_copy(
            src_ref=src, dst_ref=dst,
            send_sem=step_send_sem.at[which, step], recv_sem=step_recv_sem.at[which, step],
            device_id={"ctx": partners[orders[which][s]]}, device_id_type=MESH,
        )
        copy.start()
        started.append(copy)
        return copy

    def end_step(which, step, copy):
        copy.wait_recv()
        if step < levels:
            size = ctx_size >> (step + 1)
            offset = ctx_size - (ctx_size >> step)
            keep = pl.ds(bases[which][step + 1], size)
            acc[which, keep] = acc[which, keep] + part_recv[which, pl.ds(offset, size)].astype(F32)

    flying = [None] * (2 * cuts)
    events = [(step, which) for step in range(2 * levels) for which in range(2 * cuts)]

    def advance(step, which):
        end_step(which, step, flying[which])
        if step + 1 < 2 * levels:
            flying[which] = begin_step(which, step + 1)

    def fill(which, left, right):
        for i in range(ctx_size):
            start = ((which % cuts) * ctx_size + i) * slot_width
            acc[which, i] = ADAPTER_SCALE * nn(left, right[:, start : start + slot_width])
        flying[which] = begin_step(which, 0)

    outer = jnp.zeros((rows, low_send.shape[0]), F32)
    for g in range(kv_heads):
        head = slice(g * HEAD_SIZE, (g + 1) * HEAD_SIZE)
        for t in range(2):
            scores = nt(stacked(query, t, g), keys[t, :, head]) * scale
            scores = scores.reshape(group, half, rows) + bias[t][None]
            scores = scores.reshape(group * half, rows)
            expo = jnp.exp(scores - jnp.max(scores, axis=1, keepdims=True))
            prob = expo * (1.0 / jnp.sum(expo, axis=1, keepdims=True))
            probs[2 * g + t] = prob
            out = nn(prob.astype(BF16), values[t, :, head]).astype(BF16)
            unstack(attn, t, g, out)
        columns = slice(g * group_width, (g + 1) * group_width)
        outer = outer + nt(attn[:, columns], down[:, columns])
        if g == kv_heads - 1:
            outer_send[...] = outer.T
            outer_copy = pltpu.make_async_remote_copy(
                src_ref=outer_send, dst_ref=outer_recv, send_sem=low_sem.at[2], recv_sem=low_sem.at[3],
                device_id={"tp": 1 - tp}, device_id_type=MESH,
            )
            outer_copy.start()
        for which in range(cuts):
            if (which + 1) * kv_heads // cuts == g + 1:
                fill(which, low_t, attn)
    outer_copy.wait_recv()
    outer_sum = (outer_send[...] + outer_recv[...]).astype(BF16)
    for which in range(cuts):
        fill(cuts + which, outer_sum, grad)
    loads[8].wait()

    stores = []

    def backward(g, t):
        head = slice(g * HEAD_SIZE, (g + 1) * HEAD_SIZE)
        tail = slice(kv_width + g * HEAD_SIZE, kv_width + (g + 1) * HEAD_SIZE)
        columns = slice(g * group_width, (g + 1) * group_width)
        if t == 0:
            upstream[:, columns] = (
                upstream[:, columns].astype(F32) + ADAPTER_SCALE * nn(low[...], down[:, columns])
            ).astype(BF16)
        dout = stacked(upstream, t, g)
        out = stacked(attn, t, g)
        delta = jnp.sum(dout.astype(F32) * out.astype(F32), axis=1, keepdims=True)
        prob = probs[2 * g + t]
        dscores = (prob * (nt(dout, values[t, :, head]) - delta)).astype(BF16)
        dq = (nn(dscores, keys[t, :, head]) * scale).astype(BF16)
        unstack(dquery, t, g, dq)
        dk = tn(dscores, stacked(query, t, g)) * scale
        dv = tn(prob.astype(BF16), dout)
        back_send[t, :, head] = dk[0:half].astype(BF16)
        back_send[t, :, tail] = dv[0:half].astype(BF16)
        own_dkv[t, :, head] = dk[half:rows]
        own_dkv[t, :, tail] = dv[half:rows]
        if t == 1:
            store = pltpu.make_async_copy(
                dquery.at[:, columns], dquery_hbm.at[:, columns], store_sem.at[g]
            )
            store.start()
            stores.append(store)

    backs = []

    def send_back():
        for t in range(2):
            backs.append(
                pltpu.make_async_remote_copy(
                    src_ref=back_send.at[t], dst_ref=back_recv.at[t],
                    send_sem=back_sem.at[0, t], recv_sem=back_sem.at[1, t],
                    device_id={"ctx": me - 1 if t == 0 else me + 1}, device_id_type=MESH,
                )
            )

        @pl.when(jnp.logical_not(first))
        def _():
            backs[0].start()

        @pl.when(jnp.logical_not(last))
        def _():
            backs[1].start()

        @pl.when(first)
        def _():
            back_recv[1] = jnp.zeros(back_recv.shape[1:], BF16)

        @pl.when(last)
        def _():
            back_recv[0] = back_send[1]

    pieces = [(g, t) for g in range(kv_heads) for t in range(2)]
    for step, which in events:
        if pieces and which % 2 == 0:
            backward(*pieces.pop(0))
            if not pieces:
                send_back()
        advance(step, which)
    if pieces:
        for piece in pieces:
            backward(*piece)
        send_back()

    @pl.when(jnp.logical_not(last))
    def _():
        backs[0].wait_recv()

    @pl.when(jnp.logical_not(first))
    def _():
        backs[1].wait_recv()

    for t in range(2):
        both = own_dkv[t] + back_recv[t].astype(F32)
        dkey_ref[t * half : (t + 1) * half] = both[:, :kv_width].astype(BF16)
        dvalue_ref[t * half : (t + 1) * half] = both[:, kv_width:].astype(BF16)

    for store in stores:
        store.wait()
    for copy in started:
        copy.wait_send()
    low_copy.wait_send()
    outer_copy.wait_send()

    @pl.when(jnp.logical_not(last))
    def _():
        halos[0].wait_send()
        halos[2].wait_send()
        backs[1].wait_send()

    @pl.when(jnp.logical_not(first))
    def _():
        halos[1].wait_send()
        halos[3].wait_send()
        backs[0].wait_send()


def finish(
    dquery_from, dkey_from, dvalue_from, total,
    dquery_to, dkey_to, dvalue_to, ddown_to, dup_to, ddown, dup, sems,
):
    copies = [
        pltpu.make_async_copy(src, dst, sems.at[i])
        for i, (src, dst) in enumerate(
            [(dquery_from, dquery_to), (dkey_from, dkey_to), (dvalue_from, dvalue_to)]
        )
    ]
    for copy in copies:
        copy.start()
    cuts = total.shape[0] // 2
    slots, _, slot_width = total.shape[1:]
    for n, (block, result) in enumerate([(ddown, ddown_to), (dup, dup_to)]):
        for c in range(cuts):
            for i in range(slots):
                start = (c * slots + i) * slot_width
                block[:, start : start + slot_width] = total[n * cuts + c, i].astype(F32)
        copy = pltpu.make_async_copy(block, result, sems.at[3 + n])
        copy.start()
        copies.append(copy)
    for copy in copies:
        copy.wait()


def shards(
    query,
    key_input,
    value,
    upstream,
    output_gradient,
    down_adapter,
    up_adapter,
    document_length_list,
):
    rows, width = query.shape
    kv_width = key_input.shape[1]
    kv_heads = kv_width // HEAD_SIZE
    group = width // kv_width
    rank, model = up_adapter.shape
    half = rows // 2
    ctx_size = lax.axis_size("ctx")
    levels = ctx_size.bit_length() - 1
    cuts = max(1, min(kv_heads, width // (ctx_size * 128)))
    groups = (2 * cuts, ctx_size, rank, width // (ctx_size * cuts))
    docs = document_length_list.shape[0]
    inputs = pl.BlockSpec(memory_space=pltpu.HBM)
    anywhere = pl.BlockSpec(memory_space=pl.ANY)
    vmem = pl.BlockSpec(memory_space=pltpu.VMEM)
    dma = pltpu.SemaphoreType.DMA
    outs = pl.pallas_call(
        functools.partial(kernel, ctx_size),
        out_shape=(
            jax.ShapeDtypeStruct((rows, width), BF16),
            jax.ShapeDtypeStruct((rows, kv_width), BF16),
            jax.ShapeDtypeStruct((rows, kv_width), BF16),
            jax.ShapeDtypeStruct(groups, BF16),
        ),
        in_specs=[inputs] * 8,
        out_specs=(anywhere, vmem, vmem, vmem),
        scratch_shapes=[
            pltpu.VMEM((rows, width), BF16),
            pltpu.VMEM((rows, width), BF16),
            pltpu.VMEM((rows, model), BF16),
            pltpu.VMEM((rank, width), BF16),
            pltpu.VMEM((rank, model), BF16),
            pltpu.VMEM((2, rows, kv_width), BF16),
            pltpu.VMEM((2, rows, kv_width), BF16),
            pltpu.VMEM((2, half, rows), F32),
            pltpu.VMEM((2 * kv_heads, group * half, rows), F32),
            pltpu.VMEM((rows, width), BF16),
            pltpu.VMEM((rows, width), BF16),
            pltpu.VMEM((rank, rows), F32),
            pltpu.VMEM((rank, rows), F32),
            pltpu.VMEM((rows, rank), BF16),
            pltpu.VMEM((rank, rows), F32),
            pltpu.VMEM((rank, rows), F32),
            pltpu.VMEM((2, half, 2 * kv_width), F32),
            pltpu.VMEM((2, half, 2 * kv_width), BF16),
            pltpu.VMEM((2, half, 2 * kv_width), BF16),
            pltpu.VMEM(groups, F32),
            pltpu.VMEM(groups, BF16),
            pltpu.VMEM(groups, BF16),
            pltpu.VMEM((1, docs), jnp.int32),
            dma((10,)),
            dma((kv_heads,)),
            dma((2, 2)),
            dma((2, 2)),
            dma((4,)),
            dma((2, 2)),
            dma((2 * cuts, 2 * levels)),
            dma((2 * cuts, 2 * levels)),
        ],
        compiler_params=pltpu.CompilerParams(
            collective_id=0, has_side_effects=True, vmem_limit_bytes=63 * 1024 * 1024
        ),
    )(
        query, key_input, value, upstream, output_gradient, down_adapter.T, up_adapter,
        document_length_list[None, :],
    )
    results = (
        jax.ShapeDtypeStruct((rows, width), BF16),
        jax.ShapeDtypeStruct((rows, kv_width), BF16),
        jax.ShapeDtypeStruct((rows, kv_width), BF16),
        jax.ShapeDtypeStruct((rank, width), F32),
        jax.ShapeDtypeStruct((rank, model), F32),
    )
    dquery, dkey, dvalue, ddown, dup = pl.pallas_call(
        finish,
        out_shape=results,
        in_specs=[anywhere] * 3 + [vmem],
        out_specs=(inputs,) * 5,
        scratch_shapes=[
            pltpu.VMEM((rank, width), F32),
            pltpu.VMEM((rank, model), F32),
            dma((5,)),
        ],
    )(*outs)
    return dquery, dkey, dvalue, ddown.T, dup


def solution(mesh):
    in_specs = (
        P(("groups", "ctx"), "tp"),
        P(("groups", "ctx"), "tp"),
        P(("groups", "ctx"), "tp"),
        P(("groups", "ctx"), "tp"),
        P(("groups", "ctx"), "tp"),
        P("tp", None),
        P(None, "tp"),
        P("groups"),
    )
    out_specs = (
        P(("groups", "ctx"), "tp"),
        P(("groups", "ctx"), "tp"),
        P(("groups", "ctx"), "tp"),
        P(("groups", "tp"), None),
        P("groups", "tp"),
    )
    return jax.shard_map(shards, mesh=mesh, in_specs=in_specs, out_specs=out_specs, check_vma=False)
```

```python
import functools

import jax
import jax.numpy as jnp
from jax import lax
from jax.experimental import pallas as pl
from jax.experimental.pallas import tpu as pltpu
from jax.sharding import PartitionSpec as P

HEAD_SIZE = 128
NEG = -1e30
ADAPTER_SCALE = 0.5
MESH = pl.DeviceIdType.MESH
F32 = jnp.float32
BF16 = jnp.bfloat16


def dot(a, b, contract):
    return lax.dot_general(a, b, (contract, ((), ())), preferred_element_type=F32)


def nn(a, b):
    return dot(a, b, ((1,), (0,)))


def nt(a, b):
    return dot(a, b, ((1,), (1,)))


def tn(a, b):
    return dot(a, b, ((0,), (0,)))


def kernel(
    ctx_size, query_hbm, key_hbm, value_hbm, upstream_hbm, grad_hbm, down_hbm, up_hbm, lengths_hbm,
    dquery_hbm, dkey_ref, dvalue_ref, total,
    query, upstream, grad, down, up, keys, values, bias, probs, attn, dquery,
    low_send, low_recv, low, outer_send, outer_recv,
    own_dkv, back_send, back_recv, acc, part_send, part_recv, lengths_vmem,
    load_sem, store_sem, halo_send_sem, halo_recv_sem, low_sem, back_sem, step_send_sem, step_recv_sem,
):
    rows, width = query.shape
    half = rows // 2
    kv_width = keys.shape[2]
    kv_heads = kv_width // HEAD_SIZE
    group = width // kv_width
    group_width = group * HEAD_SIZE
    scale = HEAD_SIZE ** (-0.5)
    levels = ctx_size.bit_length() - 1
    me = lax.axis_index("ctx")
    tp = lax.axis_index("tp")
    first = me == 0
    last = me == ctx_size - 1
    bits = [(me // (1 << b)) % 2 for b in range(levels)]
    partners = [me + (1 << b) * (1 - 2 * bits[b]) for b in range(levels)]
    cuts = acc.shape[0] // 2
    swapped = list(range(levels))
    for i in range(0, levels - 1, 2):
        swapped[i], swapped[i + 1] = i + 1, i
    orders = [
        swapped if w < cuts and w % 2 == 0 or w == cuts + 1 else list(range(levels))
        for w in range(2 * cuts)
    ]

    loads = []
    for i, (src, dst) in enumerate(
        [
            (grad_hbm, grad),
            (up_hbm, up),
            (query_hbm, query),
            (key_hbm.at[0:half], keys.at[0, half:rows]),
            (key_hbm.at[half:rows], keys.at[1, half:rows]),
            (value_hbm.at[0:half], values.at[0, half:rows]),
            (value_hbm.at[half:rows], values.at[1, half:rows]),
            (down_hbm, down),
            (upstream_hbm, upstream),
            (lengths_hbm, lengths_vmem),
        ]
    ):
        copy = pltpu.make_async_copy(src, dst, load_sem.at[i])
        copy.start()
        loads.append(copy)

    barrier = pltpu.get_barrier_semaphore()
    pl.semaphore_signal(barrier, inc=1, device_id={"tp": 1 - tp}, device_id_type=MESH)
    for partner in partners:
        pl.semaphore_signal(barrier, inc=1, device_id={"ctx": partner}, device_id_type=MESH)

    @pl.when(jnp.logical_not(first))
    def _():
        pl.semaphore_signal(barrier, inc=1, device_id={"ctx": me - 1}, device_id_type=MESH)

    @pl.when(jnp.logical_not(last))
    def _():
        pl.semaphore_signal(barrier, inc=1, device_id={"ctx": me + 1}, device_id_type=MESH)

    loads[9].wait()
    lengths = lengths_vmem[...].astype(F32)
    docs = lengths.shape[1]
    line = lax.broadcasted_iota(jnp.int32, (docs, docs), 0)
    column = lax.broadcasted_iota(jnp.int32, (docs, docs), 1)
    tall = jnp.sum(jnp.where(line == column, lengths, 0.0), axis=1, keepdims=True)
    starts = jnp.sum(jnp.where(line < column, tall, 0.0), axis=0, keepdims=True)
    for t in range(2):
        stretch = me if t == 0 else 2 * ctx_size - 1 - me
        spot = (lax.broadcasted_iota(jnp.int32, (half, 1), 0) + stretch * half).astype(F32)
        begin = jnp.max(jnp.where(starts <= spot, starts, -1.0), axis=1, keepdims=True)
        key_spot = (
            lax.broadcasted_iota(jnp.int32, (half, rows), 1) + (stretch - 1) * half
        ).astype(F32)
        allowed = jnp.logical_and(key_spot >= begin, key_spot <= spot)
        bias[t] = jnp.where(allowed, 0.0, NEG)

    pl.semaphore_wait(
        barrier, 1 + levels + jnp.where(first, 0, 1) + jnp.where(last, 0, 1)
    )

    def halo(g, which, t):
        hbm, buffer = ((key_hbm, keys), (value_hbm, values))[which]
        head = slice(g * HEAD_SIZE, (g + 1) * HEAD_SIZE)
        return pltpu.make_async_remote_copy(
            src_ref=hbm.at[t * half : (t + 1) * half, head],
            dst_ref=buffer.at[t, 0:half, head],
            send_sem=halo_send_sem.at[g, which, t],
            recv_sem=halo_recv_sem.at[g, which, t],
            device_id={"ctx": me + 1 if t == 0 else me - 1},
            device_id_type=MESH,
        )

    halos = [[[halo(g, which, t) for which in range(2)] for g in range(kv_heads)] for t in range(2)]

    @pl.when(jnp.logical_not(last))
    def _():
        for pair in halos[0]:
            for copy in pair:
                copy.start()

    @pl.when(jnp.logical_not(first))
    def _():
        for pair in halos[1]:
            for copy in pair:
                copy.start()

    loads[0].wait()
    loads[1].wait()
    low_send[...] = nt(grad[...], up[...]).T
    low_copy = pltpu.make_async_remote_copy(
        src_ref=low_send, dst_ref=low_recv, send_sem=low_sem.at[0], recv_sem=low_sem.at[1],
        device_id={"tp": 1 - tp}, device_id_type=MESH,
    )
    low_copy.start()

    for i in range(2, 8):
        loads[i].wait()

    @pl.when(first)
    def _():
        keys[0, 0:half] = jnp.zeros((half, kv_width), BF16)
        values[0, 0:half] = jnp.zeros((half, kv_width), BF16)

    @pl.when(last)
    def _():
        keys[1, 0:half] = keys[0, half:rows]
        values[1, 0:half] = values[0, half:rows]

    def halo_wait(g):
        @pl.when(jnp.logical_not(first))
        def _():
            for copy in halos[0][g]:
                copy.wait_recv()

        @pl.when(jnp.logical_not(last))
        def _():
            for copy in halos[1][g]:
                copy.wait_recv()

    def stacked(ref, t, g):
        return jnp.concatenate(
            [
                ref[t * half : (t + 1) * half, g * group_width + h * HEAD_SIZE : g * group_width + (h + 1) * HEAD_SIZE]
                for h in range(group)
            ],
            axis=0,
        )

    def unstack(ref, t, g, block):
        for h in range(group):
            start = g * group_width + h * HEAD_SIZE
            ref[t * half : (t + 1) * half, start : start + HEAD_SIZE] = block[h * half : (h + 1) * half]

    slot_width = acc.shape[3]
    started = []

    def ranges(order):
        bases = [0]
        for s in range(levels):
            bases.append(bases[-1] + bits[order[s]] * (ctx_size >> (s + 1)))
        return bases

    bases = [ranges(order) for order in orders]

    def begin_step(which, step):
        if step < levels:
            s = step
            size = ctx_size >> (s + 1)
            bit = bits[orders[which][s]]
            away = bases[which][s] + (1 - bit) * size
            part_send[which, pl.ds(away, size)] = acc[which, pl.ds(away, size)].astype(BF16)
            src = part_send.at[which, pl.ds(away, size)]
            offset = ctx_size - (ctx_size >> s)
            dst = part_recv.at[which, pl.ds(offset, size)]
        else:
            s = 2 * levels - 1 - step
            size = ctx_size >> (s + 1)
            if step == levels:
                mine = bases[which][levels]
                total[which, pl.ds(mine, 1)] = acc[which, pl.ds(mine, 1)].astype(BF16)
            src = total.at[which, pl.ds(bases[which][s + 1], size)]
            dst = src
        copy = pltpu.make_async_remote_copy(
            src_ref=src, dst_ref=dst,
            send_sem=step_send_sem.at[which, step], recv_sem=step_recv_sem.at[which, step],
            device_id={"ctx": partners[orders[which][s]]}, device_id_type=MESH,
        )
        copy.start()
        started.append(copy)
        return copy

    def end_step(which, step, copy):
        copy.wait_recv()
        if step < levels:
            size = ctx_size >> (step + 1)
            offset = ctx_size - (ctx_size >> step)
            keep = pl.ds(bases[which][step + 1], size)
            acc[which, keep] = acc[which, keep] + part_recv[which, pl.ds(offset, size)].astype(F32)

    flying = [None] * (2 * cuts)
    events = [(step, which) for step in range(2 * levels) for which in range(2 * cuts)]

    def advance(step, which):
        end_step(which, step, flying[which])
        if step + 1 < 2 * levels:
            flying[which] = begin_step(which, step + 1)

    def fill(which, left, right):
        for i in range(ctx_size):
            start = ((which % cuts) * ctx_size + i) * slot_width
            acc[which, i] = ADAPTER_SCALE * nn(left, right[:, start : start + slot_width])
        flying[which] = begin_step(which, 0)

    outer = jnp.zeros((rows, low_send.shape[0]), F32)
    for g in range(kv_heads):
        head = slice(g * HEAD_SIZE, (g + 1) * HEAD_SIZE)
        halo_wait(g)
        for t in range(2):
            scores = nt(stacked(query, t, g), keys[t, :, head]) * scale
            scores = scores.reshape(group, half, rows) + bias[t][None]
            scores = scores.reshape(group * half, rows)
            expo = jnp.exp(scores - jnp.max(scores, axis=1, keepdims=True))
            prob = expo * (1.0 / jnp.sum(expo, axis=1, keepdims=True))
            probs[2 * g + t] = prob
            out = nn(prob.astype(BF16), values[t, :, head]).astype(BF16)
            unstack(attn, t, g, out)
        columns = slice(g * group_width, (g + 1) * group_width)
        outer = outer + nt(attn[:, columns], down[:, columns])
        if g == kv_heads - 1:
            outer_send[...] = outer.T
            outer_copy = pltpu.make_async_remote_copy(
                src_ref=outer_send, dst_ref=outer_recv, send_sem=low_sem.at[2], recv_sem=low_sem.at[3],
                device_id={"tp": 1 - tp}, device_id_type=MESH,
            )
            outer_copy.start()
        if g == 0:
            low_copy.wait_recv()
            low_t = (low_send[...] + low_recv[...]).astype(BF16)
            low[...] = (low_send[...] + low_recv[...]).T.astype(BF16)
        for which in range(cuts):
            if (which + 1) * kv_heads // cuts == g + 1:
                fill(which, low_t, attn)
    outer_copy.wait_recv()
    outer_sum = (outer_send[...] + outer_recv[...]).astype(BF16)
    for which in range(cuts):
        fill(cuts + which, outer_sum, grad)
    loads[8].wait()

    stores = []

    def backward(g, t):
        head = slice(g * HEAD_SIZE, (g + 1) * HEAD_SIZE)
        tail = slice(kv_width + g * HEAD_SIZE, kv_width + (g + 1) * HEAD_SIZE)
        columns = slice(g * group_width, (g + 1) * group_width)
        if t == 0:
            upstream[:, columns] = (
                upstream[:, columns].astype(F32) + ADAPTER_SCALE * nn(low[...], down[:, columns])
            ).astype(BF16)
        dout = stacked(upstream, t, g)
        out = stacked(attn, t, g)
        delta = jnp.sum(dout.astype(F32) * out.astype(F32), axis=1, keepdims=True)
        prob = probs[2 * g + t]
        dscores = (prob * (nt(dout, values[t, :, head]) - delta)).astype(BF16)
        dq = (nn(dscores, keys[t, :, head]) * scale).astype(BF16)
        unstack(dquery, t, g, dq)
        dk = tn(dscores, stacked(query, t, g)) * scale
        dv = tn(prob.astype(BF16), dout)
        back_send[t, :, head] = dk[0:half].astype(BF16)
        back_send[t, :, tail] = dv[0:half].astype(BF16)
        own_dkv[t, :, head] = dk[half:rows]
        own_dkv[t, :, tail] = dv[half:rows]
        if t == 1:
            store = pltpu.make_async_copy(
                dquery.at[:, columns], dquery_hbm.at[:, columns], store_sem.at[g]
            )
            store.start()
            stores.append(store)

    backs = []

    def send_back():
        for t in range(2):
            backs.append(
                pltpu.make_async_remote_copy(
                    src_ref=back_send.at[t], dst_ref=back_recv.at[t],
                    send_sem=back_sem.at[0, t], recv_sem=back_sem.at[1, t],
                    device_id={"ctx": me - 1 if t == 0 else me + 1}, device_id_type=MESH,
                )
            )

        @pl.when(jnp.logical_not(first))
        def _():
            backs[0].start()

        @pl.when(jnp.logical_not(last))
        def _():
            backs[1].start()

        @pl.when(first)
        def _():
            back_recv[1] = jnp.zeros(back_recv.shape[1:], BF16)

        @pl.when(last)
        def _():
            back_recv[0] = back_send[1]

    pieces = [(g, t) for g in range(kv_heads) for t in range(2)]
    for step, which in events:
        if pieces and (which % 2 == 0 or step > 1):
            backward(*pieces.pop(0))
            if not pieces:
                send_back()
        advance(step, which)
    if pieces:
        for piece in pieces:
            backward(*piece)
        send_back()

    @pl.when(jnp.logical_not(last))
    def _():
        backs[0].wait_recv()

    @pl.when(jnp.logical_not(first))
    def _():
        backs[1].wait_recv()

    for t in range(2):
        both = own_dkv[t] + back_recv[t].astype(F32)
        dkey_ref[t * half : (t + 1) * half] = both[:, :kv_width].astype(BF16)
        dvalue_ref[t * half : (t + 1) * half] = both[:, kv_width:].astype(BF16)

    for store in stores:
        store.wait()
    for copy in started:
        copy.wait_send()
    low_copy.wait_send()
    outer_copy.wait_send()

    @pl.when(jnp.logical_not(last))
    def _():
        for pair in halos[0]:
            for copy in pair:
                copy.wait_send()
        backs[1].wait_send()

    @pl.when(jnp.logical_not(first))
    def _():
        for pair in halos[1]:
            for copy in pair:
                copy.wait_send()
        backs[0].wait_send()


def finish(
    dquery_from, dkey_from, dvalue_from, total_from,
    dquery_to, dkey_to, dvalue_to, ddown_to, dup_to,
    dquery, dkey, dvalue, total, ddown, dup, in_sems, out_sems,
):
    strip = dquery.shape[0] // 4
    moves = [
        (total_from, total, None),
        (dkey_from, dkey, dkey_to),
        (dvalue_from, dvalue, dvalue_to),
    ] + [
        (dquery_from.at[part], dquery.at[part], dquery_to.at[part])
        for part in [pl.ds(i * strip, strip) for i in range(4)]
    ]
    ins = [pltpu.make_async_copy(m[0], m[1], in_sems.at[i]) for i, m in enumerate(moves)]
    for copy in ins:
        copy.start()
    outs = []
    ins[0].wait()
    cuts = total.shape[0] // 2
    slots, _, slot_width = total.shape[1:]
    for n, (block, result) in enumerate([(ddown, ddown_to), (dup, dup_to)]):
        for c in range(cuts):
            for i in range(slots):
                start = (c * slots + i) * slot_width
                block[:, start : start + slot_width] = total[n * cuts + c, i].astype(F32)
        outs.append(pltpu.make_async_copy(block, result, out_sems.at[n]))
        outs[-1].start()
    for i in range(1, len(moves)):
        ins[i].wait()
        outs.append(pltpu.make_async_copy(moves[i][1], moves[i][2], out_sems.at[i + 1]))
        outs[-1].start()
    for copy in outs:
        copy.wait()


def shards(
    query,
    key_input,
    value,
    upstream,
    output_gradient,
    down_adapter,
    up_adapter,
    document_length_list,
):
    rows, width = query.shape
    kv_width = key_input.shape[1]
    kv_heads = kv_width // HEAD_SIZE
    group = width // kv_width
    rank, model = up_adapter.shape
    half = rows // 2
    ctx_size = lax.axis_size("ctx")
    levels = ctx_size.bit_length() - 1
    cuts = max(1, min(kv_heads, width // (ctx_size * 128)))
    groups = (2 * cuts, ctx_size, rank, width // (ctx_size * cuts))
    docs = document_length_list.shape[0]
    inputs = pl.BlockSpec(memory_space=pltpu.HBM)
    anywhere = pl.BlockSpec(memory_space=pl.ANY)
    vmem = pl.BlockSpec(memory_space=pltpu.VMEM)
    dma = pltpu.SemaphoreType.DMA
    outs = pl.pallas_call(
        functools.partial(kernel, ctx_size),
        out_shape=(
            jax.ShapeDtypeStruct((rows, width), BF16),
            jax.ShapeDtypeStruct((rows, kv_width), BF16),
            jax.ShapeDtypeStruct((rows, kv_width), BF16),
            jax.ShapeDtypeStruct(groups, BF16),
        ),
        in_specs=[inputs] * 8,
        out_specs=(anywhere, vmem, vmem, vmem),
        scratch_shapes=[
            pltpu.VMEM((rows, width), BF16),
            pltpu.VMEM((rows, width), BF16),
            pltpu.VMEM((rows, model), BF16),
            pltpu.VMEM((rank, width), BF16),
            pltpu.VMEM((rank, model), BF16),
            pltpu.VMEM((2, rows, kv_width), BF16),
            pltpu.VMEM((2, rows, kv_width), BF16),
            pltpu.VMEM((2, half, rows), F32),
            pltpu.VMEM((2 * kv_heads, group * half, rows), F32),
            pltpu.VMEM((rows, width), BF16),
            pltpu.VMEM((rows, width), BF16),
            pltpu.VMEM((rank, rows), F32),
            pltpu.VMEM((rank, rows), F32),
            pltpu.VMEM((rows, rank), BF16),
            pltpu.VMEM((rank, rows), F32),
            pltpu.VMEM((rank, rows), F32),
            pltpu.VMEM((2, half, 2 * kv_width), F32),
            pltpu.VMEM((2, half, 2 * kv_width), BF16),
            pltpu.VMEM((2, half, 2 * kv_width), BF16),
            pltpu.VMEM(groups, F32),
            pltpu.VMEM(groups, BF16),
            pltpu.VMEM(groups, BF16),
            pltpu.VMEM((1, docs), jnp.int32),
            dma((10,)),
            dma((kv_heads,)),
            dma((kv_heads, 2, 2)),
            dma((kv_heads, 2, 2)),
            dma((4,)),
            dma((2, 2)),
            dma((2 * cuts, 2 * levels)),
            dma((2 * cuts, 2 * levels)),
        ],
        compiler_params=pltpu.CompilerParams(
            collective_id=0, has_side_effects=True, vmem_limit_bytes=63 * 1024 * 1024
        ),
    )(
        query, key_input, value, upstream, output_gradient, down_adapter.T, up_adapter,
        document_length_list[None, :],
    )
    results = (
        jax.ShapeDtypeStruct((rows, width), BF16),
        jax.ShapeDtypeStruct((rows, kv_width), BF16),
        jax.ShapeDtypeStruct((rows, kv_width), BF16),
        jax.ShapeDtypeStruct((rank, width), F32),
        jax.ShapeDtypeStruct((rank, model), F32),
    )
    dquery, dkey, dvalue, ddown, dup = pl.pallas_call(
        finish,
        out_shape=results,
        in_specs=[anywhere] * 4,
        out_specs=(inputs,) * 5,
        scratch_shapes=[
            pltpu.VMEM((rows, width), BF16),
            pltpu.VMEM((rows, kv_width), BF16),
            pltpu.VMEM((rows, kv_width), BF16),
            pltpu.VMEM(groups, BF16),
            pltpu.VMEM((rank, width), F32),
            pltpu.VMEM((rank, model), F32),
            dma((7,)),
            dma((8,)),
        ],
        compiler_params=pltpu.CompilerParams(vmem_limit_bytes=63 * 1024 * 1024),
    )(*outs)
    return dquery, dkey, dvalue, ddown.T, dup


def solution(mesh):
    in_specs = (
        P(("groups", "ctx"), "tp"),
        P(("groups", "ctx"), "tp"),
        P(("groups", "ctx"), "tp"),
        P(("groups", "ctx"), "tp"),
        P(("groups", "ctx"), "tp"),
        P("tp", None),
        P(None, "tp"),
        P("groups"),
    )
    out_specs = (
        P(("groups", "ctx"), "tp"),
        P(("groups", "ctx"), "tp"),
        P(("groups", "ctx"), "tp"),
        P(("groups", "tp"), None),
        P("groups", "tp"),
    )
    return jax.shard_map(shards, mesh=mesh, in_specs=in_specs, out_specs=out_specs, check_vma=False)
```

```python
import functools

import jax
import jax.numpy as jnp
from jax import lax
from jax.experimental import pallas as pl
from jax.experimental.pallas import tpu as pltpu
from jax.sharding import PartitionSpec as P

HEAD_SIZE = 128
NEG = -1e30
ADAPTER_SCALE = 0.5
MESH = pl.DeviceIdType.MESH
F32 = jnp.float32
BF16 = jnp.bfloat16


def dot(a, b, contract):
    return lax.dot_general(a, b, (contract, ((), ())), preferred_element_type=F32)


def nn(a, b):
    return dot(a, b, ((1,), (0,)))


def nt(a, b):
    return dot(a, b, ((1,), (1,)))


def tn(a, b):
    return dot(a, b, ((0,), (0,)))


def kernel(
    ctx_size, query_hbm, key_hbm, value_hbm, upstream_hbm, grad_hbm, down_hbm, up_hbm, lengths_hbm,
    dquery_hbm, dkey_ref, dvalue_ref, total,
    query, upstream, grad, down, up, keys, values, bias, probs, attn, dquery,
    low_send, low_recv, low, outer_send, outer_recv,
    own_dkv, back_send, back_recv, acc, part_send, part_recv, lengths_vmem,
    load_sem, store_sem, halo_send_sem, halo_recv_sem, low_sem, back_sem, step_send_sem, step_recv_sem,
):
    rows, width = query.shape
    half = rows // 2
    kv_width = keys.shape[2]
    kv_heads = kv_width // HEAD_SIZE
    group = width // kv_width
    group_width = group * HEAD_SIZE
    scale = HEAD_SIZE ** (-0.5)
    levels = ctx_size.bit_length() - 1
    me = lax.axis_index("ctx")
    tp = lax.axis_index("tp")
    first = me == 0
    last = me == ctx_size - 1
    bits = [(me // (1 << b)) % 2 for b in range(levels)]
    partners = [me + (1 << b) * (1 - 2 * bits[b]) for b in range(levels)]
    cuts = acc.shape[0] // 2
    swapped = list(range(levels))
    for i in range(0, levels - 1, 2):
        swapped[i], swapped[i + 1] = i + 1, i
    orders = [
        swapped if w % 2 == 0 else list(range(levels))
        for w in range(2 * cuts)
    ]

    loads = []
    for i, (src, dst) in enumerate(
        [
            (grad_hbm, grad),
            (up_hbm, up),
            (query_hbm, query),
            (key_hbm.at[0:half], keys.at[0, half:rows]),
            (key_hbm.at[half:rows], keys.at[1, half:rows]),
            (value_hbm.at[0:half], values.at[0, half:rows]),
            (value_hbm.at[half:rows], values.at[1, half:rows]),
            (down_hbm, down),
            (upstream_hbm, upstream),
            (lengths_hbm, lengths_vmem),
        ]
    ):
        copy = pltpu.make_async_copy(src, dst, load_sem.at[i])
        copy.start()
        loads.append(copy)

    barrier = pltpu.get_barrier_semaphore()
    pl.semaphore_signal(barrier, inc=1, device_id={"tp": 1 - tp}, device_id_type=MESH)
    for partner in partners:
        pl.semaphore_signal(barrier, inc=1, device_id={"ctx": partner}, device_id_type=MESH)

    @pl.when(jnp.logical_not(first))
    def _():
        pl.semaphore_signal(barrier, inc=1, device_id={"ctx": me - 1}, device_id_type=MESH)

    @pl.when(jnp.logical_not(last))
    def _():
        pl.semaphore_signal(barrier, inc=1, device_id={"ctx": me + 1}, device_id_type=MESH)

    loads[9].wait()
    lengths = lengths_vmem[...].astype(F32)
    docs = lengths.shape[1]
    line = lax.broadcasted_iota(jnp.int32, (docs, docs), 0)
    column = lax.broadcasted_iota(jnp.int32, (docs, docs), 1)
    tall = jnp.sum(jnp.where(line == column, lengths, 0.0), axis=1, keepdims=True)
    starts = jnp.sum(jnp.where(line < column, tall, 0.0), axis=0, keepdims=True)
    for t in range(2):
        stretch = me if t == 0 else 2 * ctx_size - 1 - me
        spot = (lax.broadcasted_iota(jnp.int32, (half, 1), 0) + stretch * half).astype(F32)
        begin = jnp.max(jnp.where(starts <= spot, starts, -1.0), axis=1, keepdims=True)
        key_spot = (
            lax.broadcasted_iota(jnp.int32, (half, rows), 1) + (stretch - 1) * half
        ).astype(F32)
        allowed = jnp.logical_and(key_spot >= begin, key_spot <= spot)
        bias[t] = jnp.where(allowed, 0.0, NEG)

    pl.semaphore_wait(
        barrier, 1 + levels + jnp.where(first, 0, 1) + jnp.where(last, 0, 1)
    )

    def halo(g, which, t):
        hbm, buffer = ((key_hbm, keys), (value_hbm, values))[which]
        head = slice(g * HEAD_SIZE, (g + 1) * HEAD_SIZE)
        return pltpu.make_async_remote_copy(
            src_ref=hbm.at[t * half : (t + 1) * half, head],
            dst_ref=buffer.at[t, 0:half, head],
            send_sem=halo_send_sem.at[g, which, t],
            recv_sem=halo_recv_sem.at[g, which, t],
            device_id={"ctx": me + 1 if t == 0 else me - 1},
            device_id_type=MESH,
        )

    halos = [[[halo(g, which, t) for which in range(2)] for g in range(kv_heads)] for t in range(2)]

    @pl.when(jnp.logical_not(last))
    def _():
        for pair in halos[0]:
            for copy in pair:
                copy.start()

    @pl.when(jnp.logical_not(first))
    def _():
        for pair in halos[1]:
            for copy in pair:
                copy.start()

    loads[0].wait()
    loads[1].wait()
    low_send[...] = nt(grad[...], up[...]).T
    low_copy = pltpu.make_async_remote_copy(
        src_ref=low_send, dst_ref=low_recv, send_sem=low_sem.at[0], recv_sem=low_sem.at[1],
        device_id={"tp": 1 - tp}, device_id_type=MESH,
    )
    low_copy.start()

    for i in range(2, 8):
        loads[i].wait()

    @pl.when(first)
    def _():
        keys[0, 0:half] = jnp.zeros((half, kv_width), BF16)
        values[0, 0:half] = jnp.zeros((half, kv_width), BF16)

    @pl.when(last)
    def _():
        keys[1, 0:half] = keys[0, half:rows]
        values[1, 0:half] = values[0, half:rows]

    def halo_wait(g):
        @pl.when(jnp.logical_not(first))
        def _():
            for copy in halos[0][g]:
                copy.wait_recv()

        @pl.when(jnp.logical_not(last))
        def _():
            for copy in halos[1][g]:
                copy.wait_recv()

    def stacked(ref, t, g):
        return jnp.concatenate(
            [
                ref[t * half : (t + 1) * half, g * group_width + h * HEAD_SIZE : g * group_width + (h + 1) * HEAD_SIZE]
                for h in range(group)
            ],
            axis=0,
        )

    def unstack(ref, t, g, block):
        for h in range(group):
            start = g * group_width + h * HEAD_SIZE
            ref[t * half : (t + 1) * half, start : start + HEAD_SIZE] = block[h * half : (h + 1) * half]

    slot_width = acc.shape[3]
    started = []

    def ranges(order):
        bases = [0]
        for s in range(levels):
            bases.append(bases[-1] + bits[order[s]] * (ctx_size >> (s + 1)))
        return bases

    bases = [ranges(order) for order in orders]

    def begin_step(which, step):
        if step < levels:
            s = step
            size = ctx_size >> (s + 1)
            bit = bits[orders[which][s]]
            away = bases[which][s] + (1 - bit) * size
            part_send[which, pl.ds(away, size)] = acc[which, pl.ds(away, size)].astype(BF16)
            src = part_send.at[which, pl.ds(away, size)]
            offset = ctx_size - (ctx_size >> s)
            dst = part_recv.at[which, pl.ds(offset, size)]
        else:
            s = 2 * levels - 1 - step
            size = ctx_size >> (s + 1)
            if step == levels:
                mine = bases[which][levels]
                total[which, pl.ds(mine, 1)] = acc[which, pl.ds(mine, 1)].astype(BF16)
            src = total.at[which, pl.ds(bases[which][s + 1], size)]
            dst = src
        copy = pltpu.make_async_remote_copy(
            src_ref=src, dst_ref=dst,
            send_sem=step_send_sem.at[which, step], recv_sem=step_recv_sem.at[which, step],
            device_id={"ctx": partners[orders[which][s]]}, device_id_type=MESH,
        )
        copy.start()
        started.append(copy)
        return copy

    def end_step(which, step, copy):
        copy.wait_recv()
        if step < levels:
            size = ctx_size >> (step + 1)
            offset = ctx_size - (ctx_size >> step)
            keep = pl.ds(bases[which][step + 1], size)
            acc[which, keep] = acc[which, keep] + part_recv[which, pl.ds(offset, size)].astype(F32)

    flying = [None] * (2 * cuts)
    events = [(step, which) for step in range(2 * levels) for which in range(2 * cuts)]

    def advance(step, which):
        end_step(which, step, flying[which])
        if step + 1 < 2 * levels:
            flying[which] = begin_step(which, step + 1)

    def fill(which, left, right):
        for i in range(ctx_size):
            start = ((which % cuts) * ctx_size + i) * slot_width
            acc[which, i] = ADAPTER_SCALE * nn(left, right[:, start : start + slot_width])
        flying[which] = begin_step(which, 0)

    outer = jnp.zeros((rows, low_send.shape[0]), F32)
    for g in range(kv_heads):
        head = slice(g * HEAD_SIZE, (g + 1) * HEAD_SIZE)
        halo_wait(g)
        for t in range(2):
            scores = nt(stacked(query, t, g), keys[t, :, head]) * scale
            scores = scores.reshape(group, half, rows) + bias[t][None]
            scores = scores.reshape(group * half, rows)
            expo = jnp.exp(scores - jnp.max(scores, axis=1, keepdims=True))
            prob = expo * (1.0 / jnp.sum(expo, axis=1, keepdims=True))
            probs[2 * g + t] = prob
            out = nn(prob.astype(BF16), values[t, :, head]).astype(BF16)
            unstack(attn, t, g, out)
        columns = slice(g * group_width, (g + 1) * group_width)
        outer = outer + nt(attn[:, columns], down[:, columns])
        if g == kv_heads - 1:
            outer_send[...] = outer.T
            outer_copy = pltpu.make_async_remote_copy(
                src_ref=outer_send, dst_ref=outer_recv, send_sem=low_sem.at[2], recv_sem=low_sem.at[3],
                device_id={"tp": 1 - tp}, device_id_type=MESH,
            )
            outer_copy.start()
        if g == 0:
            low_copy.wait_recv()
            low_t = (low_send[...] + low_recv[...]).astype(BF16)
            low[...] = (low_send[...] + low_recv[...]).T.astype(BF16)
        for which in range(cuts):
            if (which + 1) * kv_heads // cuts == g + 1:
                fill(which, low_t, attn)
    stores = []

    def backward(g, t):
        head = slice(g * HEAD_SIZE, (g + 1) * HEAD_SIZE)
        tail = slice(kv_width + g * HEAD_SIZE, kv_width + (g + 1) * HEAD_SIZE)
        columns = slice(g * group_width, (g + 1) * group_width)
        if t == 0:
            upstream[:, columns] = (
                upstream[:, columns].astype(F32) + ADAPTER_SCALE * nn(low[...], down[:, columns])
            ).astype(BF16)
        dout = stacked(upstream, t, g)
        out = stacked(attn, t, g)
        delta = jnp.sum(dout.astype(F32) * out.astype(F32), axis=1, keepdims=True)
        prob = probs[2 * g + t]
        dscores = (prob * (nt(dout, values[t, :, head]) - delta)).astype(BF16)
        dq = (nn(dscores, keys[t, :, head]) * scale).astype(BF16)
        unstack(dquery, t, g, dq)
        dk = tn(dscores, stacked(query, t, g)) * scale
        dv = tn(prob.astype(BF16), dout)
        back_send[t, :, head] = dk[0:half].astype(BF16)
        back_send[t, :, tail] = dv[0:half].astype(BF16)
        own_dkv[t, :, head] = dk[half:rows]
        own_dkv[t, :, tail] = dv[half:rows]
        if t == 1:
            store = pltpu.make_async_copy(
                dquery.at[:, columns], dquery_hbm.at[:, columns], store_sem.at[g]
            )
            store.start()
            stores.append(store)

    pieces = [(g, t) for g in range(kv_heads) for t in range(2)]
    loads[8].wait()
    backward(*pieces.pop(0))
    outer_copy.wait_recv()
    outer_sum = (outer_send[...] + outer_recv[...]).astype(BF16)
    for which in range(cuts):
        fill(cuts + which, outer_sum, grad)
    backs = []

    def send_back():
        for t in range(2):
            backs.append(
                pltpu.make_async_remote_copy(
                    src_ref=back_send.at[t], dst_ref=back_recv.at[t],
                    send_sem=back_sem.at[0, t], recv_sem=back_sem.at[1, t],
                    device_id={"ctx": me - 1 if t == 0 else me + 1}, device_id_type=MESH,
                )
            )

        @pl.when(jnp.logical_not(first))
        def _():
            backs[0].start()

        @pl.when(jnp.logical_not(last))
        def _():
            backs[1].start()

        @pl.when(first)
        def _():
            back_recv[1] = jnp.zeros(back_recv.shape[1:], BF16)

        @pl.when(last)
        def _():
            back_recv[0] = back_send[1]

    for step, which in events:
        if pieces and (which % 2 == 0 or step > 1):
            backward(*pieces.pop(0))
            if not pieces:
                send_back()
        advance(step, which)
    if pieces:
        for piece in pieces:
            backward(*piece)
        send_back()

    @pl.when(jnp.logical_not(last))
    def _():
        backs[0].wait_recv()

    @pl.when(jnp.logical_not(first))
    def _():
        backs[1].wait_recv()

    for t in range(2):
        both = own_dkv[t] + back_recv[t].astype(F32)
        dkey_ref[t * half : (t + 1) * half] = both[:, :kv_width].astype(BF16)
        dvalue_ref[t * half : (t + 1) * half] = both[:, kv_width:].astype(BF16)

    for store in stores:
        store.wait()
    for copy in started:
        copy.wait_send()
    low_copy.wait_send()
    outer_copy.wait_send()

    @pl.when(jnp.logical_not(last))
    def _():
        for pair in halos[0]:
            for copy in pair:
                copy.wait_send()
        backs[1].wait_send()

    @pl.when(jnp.logical_not(first))
    def _():
        for pair in halos[1]:
            for copy in pair:
                copy.wait_send()
        backs[0].wait_send()


def finish(
    dquery_from, dkey_from, dvalue_from, total_from,
    dquery_to, dkey_to, dvalue_to, ddown_to, dup_to,
    dquery, dkey, dvalue, total, ddown, dup, in_sems, out_sems,
):
    strip = dquery.shape[0] // 4
    moves = [
        (total_from, total, None),
        (dkey_from, dkey, dkey_to),
        (dvalue_from, dvalue, dvalue_to),
    ] + [
        (dquery_from.at[part], dquery.at[part], dquery_to.at[part])
        for part in [pl.ds(i * strip, strip) for i in range(4)]
    ]
    ins = [pltpu.make_async_copy(m[0], m[1], in_sems.at[i]) for i, m in enumerate(moves)]
    for copy in ins:
        copy.start()
    outs = []
    ins[0].wait()
    cuts = total.shape[0] // 2
    slots, _, slot_width = total.shape[1:]
    for n, (block, result) in enumerate([(ddown, ddown_to), (dup, dup_to)]):
        for c in range(cuts):
            for i in range(slots):
                start = (c * slots + i) * slot_width
                block[:, start : start + slot_width] = total[n * cuts + c, i].astype(F32)
        outs.append(pltpu.make_async_copy(block, result, out_sems.at[n]))
        outs[-1].start()
    for i in range(1, len(moves)):
        ins[i].wait()
        outs.append(pltpu.make_async_copy(moves[i][1], moves[i][2], out_sems.at[i + 1]))
        outs[-1].start()
    for copy in outs:
        copy.wait()


def shards(
    query,
    key_input,
    value,
    upstream,
    output_gradient,
    down_adapter,
    up_adapter,
    document_length_list,
):
    rows, width = query.shape
    kv_width = key_input.shape[1]
    kv_heads = kv_width // HEAD_SIZE
    group = width // kv_width
    rank, model = up_adapter.shape
    half = rows // 2
    ctx_size = lax.axis_size("ctx")
    levels = ctx_size.bit_length() - 1
    cuts = max(1, min(kv_heads, width // (ctx_size * 128)))
    groups = (2 * cuts, ctx_size, rank, width // (ctx_size * cuts))
    docs = document_length_list.shape[0]
    inputs = pl.BlockSpec(memory_space=pltpu.HBM)
    anywhere = pl.BlockSpec(memory_space=pl.ANY)
    vmem = pl.BlockSpec(memory_space=pltpu.VMEM)
    dma = pltpu.SemaphoreType.DMA
    outs = pl.pallas_call(
        functools.partial(kernel, ctx_size),
        out_shape=(
            jax.ShapeDtypeStruct((rows, width), BF16),
            jax.ShapeDtypeStruct((rows, kv_width), BF16),
            jax.ShapeDtypeStruct((rows, kv_width), BF16),
            jax.ShapeDtypeStruct(groups, BF16),
        ),
        in_specs=[inputs] * 8,
        out_specs=(anywhere, vmem, vmem, vmem),
        scratch_shapes=[
            pltpu.VMEM((rows, width), BF16),
            pltpu.VMEM((rows, width), BF16),
            pltpu.VMEM((rows, model), BF16),
            pltpu.VMEM((rank, width), BF16),
            pltpu.VMEM((rank, model), BF16),
            pltpu.VMEM((2, rows, kv_width), BF16),
            pltpu.VMEM((2, rows, kv_width), BF16),
            pltpu.VMEM((2, half, rows), F32),
            pltpu.VMEM((2 * kv_heads, group * half, rows), F32),
            pltpu.VMEM((rows, width), BF16),
            pltpu.VMEM((rows, width), BF16),
            pltpu.VMEM((rank, rows), F32),
            pltpu.VMEM((rank, rows), F32),
            pltpu.VMEM((rows, rank), BF16),
            pltpu.VMEM((rank, rows), F32),
            pltpu.VMEM((rank, rows), F32),
            pltpu.VMEM((2, half, 2 * kv_width), F32),
            pltpu.VMEM((2, half, 2 * kv_width), BF16),
            pltpu.VMEM((2, half, 2 * kv_width), BF16),
            pltpu.VMEM(groups, F32),
            pltpu.VMEM(groups, BF16),
            pltpu.VMEM(groups, BF16),
            pltpu.VMEM((1, docs), jnp.int32),
            dma((10,)),
            dma((kv_heads,)),
            dma((kv_heads, 2, 2)),
            dma((kv_heads, 2, 2)),
            dma((4,)),
            dma((2, 2)),
            dma((2 * cuts, 2 * levels)),
            dma((2 * cuts, 2 * levels)),
        ],
        compiler_params=pltpu.CompilerParams(
            collective_id=0, has_side_effects=True, vmem_limit_bytes=63 * 1024 * 1024
        ),
    )(
        query, key_input, value, upstream, output_gradient, down_adapter.T, up_adapter,
        document_length_list[None, :],
    )
    results = (
        jax.ShapeDtypeStruct((rows, width), BF16),
        jax.ShapeDtypeStruct((rows, kv_width), BF16),
        jax.ShapeDtypeStruct((rows, kv_width), BF16),
        jax.ShapeDtypeStruct((rank, width), F32),
        jax.ShapeDtypeStruct((rank, model), F32),
    )
    dquery, dkey, dvalue, ddown, dup = pl.pallas_call(
        finish,
        out_shape=results,
        in_specs=[anywhere] * 4,
        out_specs=(inputs,) * 5,
        scratch_shapes=[
            pltpu.VMEM((rows, width), BF16),
            pltpu.VMEM((rows, kv_width), BF16),
            pltpu.VMEM((rows, kv_width), BF16),
            pltpu.VMEM(groups, BF16),
            pltpu.VMEM((rank, width), F32),
            pltpu.VMEM((rank, model), F32),
            dma((7,)),
            dma((8,)),
        ],
        compiler_params=pltpu.CompilerParams(vmem_limit_bytes=63 * 1024 * 1024),
    )(*outs)
    return dquery, dkey, dvalue, ddown.T, dup


def solution(mesh):
    in_specs = (
        P(("groups", "ctx"), "tp"),
        P(("groups", "ctx"), "tp"),
        P(("groups", "ctx"), "tp"),
        P(("groups", "ctx"), "tp"),
        P(("groups", "ctx"), "tp"),
        P("tp", None),
        P(None, "tp"),
        P("groups"),
    )
    out_specs = (
        P(("groups", "ctx"), "tp"),
        P(("groups", "ctx"), "tp"),
        P(("groups", "ctx"), "tp"),
        P(("groups", "tp"), None),
        P("groups", "tp"),
    )
    return jax.shard_map(shards, mesh=mesh, in_specs=in_specs, out_specs=out_specs, check_vma=False)
```
